32 devices in a mesh: section: 4 (over x, core), tp: 8 (over z, y).
Axes of the slice: x: 2, y: 2, z: 4, core: 2. Of those that a mesh axis runs over, the one named last changes fastest.
Arguments:
- query: bfloat16 [4, 2, 1024, 4096], P('section', None, 'tp'), may hold values from -6 to 6
- keys_values: bfloat16 [4, 2, 2, 1024, 512], P('section', None, None, 'tp'), may hold values from -6 to 6
- grad_out: bfloat16 [4, 2, 1024, 4096], P('section', None, 'tp'), may hold values from -6 to 6
- fwd_query: bfloat16 [4, 2, 1024, 4096], P('section', None, 'tp'), may hold values from -6 to 6
- fwd_keys_values: bfloat16 [4, 2, 2, 1024, 512], P('section', None, None, 'tp'), may hold values from -6 to 6
- held_out: bfloat16 [4, 2, 1024, 4096], P('section', None, None, 'tp'), may hold values from -4 to 4
- evict: int32 [2, 2, 2], replicated, may hold values from 0 to 1
Outputs:
- passed_on: bfloat16 [4, 2, 1024, 4096], P('section', None, 'tp')
- grad_query: bfloat16 [4, 2, 1024, 4096], P('section', None, 'tp')
- grad_keys_values: bfloat16 [4, 2, 2, 1024, 512], P('section', None, None, 'tp')
- mirror_out: bfloat16 [4, 2, 1024, 4096], P('section', None, None, 'tp')
The draws below stay inside these ranges and needn't reach their ends.
All inputs are finite; a program needn't handle non-finite values.
Results may differ from the reference program's by a relative error of at most 0.0057.
Values may be sent and summed in bfloat16 or wider, within the bound.
A program may use at most 128 MiB of HBM per device.

```python
import math
import jax
import jax.numpy as jnp
from jax import lax

HEADS = 32
KV_HEADS = 4
HD = 128
SEQ = 1024
MB = 2
N_SECTION = 4


def touch_ends(result, own_key, smallest, high):
    extent = result.shape
    index_at = [jax.random.randint(jax.random.fold_in(own_key, axis), (), 0, extent[axis]) for axis in range(len(extent))]
    result = result.at[tuple(index_at)].set(smallest)
    longest = extent.index(max(extent))
    index_at[longest] = (index_at[longest] + 1) % extent[longest]
    return result.at[tuple(index_at)].set(high)


def levels(own_key, dims, split, smallest, largest):
    loudness = 1.0
    for axis_at, shards_of in split:
        heights = jax.random.uniform(jax.random.fold_in(jax.random.fold_in(own_key, 6), axis_at), (shards_of,), jnp.float32, smallest / len(split), largest / len(split))
        loudness = loudness * jnp.repeat(jnp.exp(heights), dims[axis_at] // shards_of).reshape((-1,) + (1,) * (len(dims) - 1 - axis_at))
    return loudness


def centred(stream_key, dims, spread, limit, pieces=(), held_as=jnp.bfloat16):
    gain = levels(stream_key, dims, pieces, -0.22, 0.18) if pieces else 1.0
    drawn = jax.random.normal(stream_key, dims, jnp.float32) * spread * gain
    return jnp.minimum(jnp.maximum(drawn, -limit), limit).astype(held_as)


def setup_inputs(seed: int = 0) -> dict:
    seeds = jax.random.split(jax.random.key(seed), 8)
    return {
        "query": centred(seeds[0], (N_SECTION, MB, SEQ, HEADS * HD), 1.0, 6.0, ((0, 4), (2, 8))),
        "keys_values": centred(seeds[1], (N_SECTION, MB, 2, SEQ, KV_HEADS * HD), 1.0, 6.0, ((0, 4), (3, 8))),
        "grad_out": centred(seeds[2], (N_SECTION, MB, SEQ, HEADS * HD), 1.0, 6.0, ((0, 4), (2, 8))),
        "fwd_query": centred(seeds[3], (N_SECTION, MB, SEQ, HEADS * HD), 1.0, 6.0, ((0, 4), (2, 8))),
        "fwd_keys_values": centred(seeds[4], (N_SECTION, MB, 2, SEQ, KV_HEADS * HD), 1.0, 6.0, ((0, 4), (3, 8))),
        "held_out": centred(seeds[5], (N_SECTION, MB, SEQ, HEADS * HD), 0.25, 4.0, ((0, 4), (3, 8))),
        "evict": touch_ends(jax.random.randint(seeds[6], (N_SECTION // 2, 2, MB), 0, 2), jax.random.fold_in(seeds[6], 1), 0, 1).astype(jnp.int32),
    }


def attend(query, keys, values):
    scale = 1.0 / math.sqrt(HD)
    scores = jnp.dot(query, keys.T, preferred_element_type=jnp.float32) * scale
    rows = jnp.arange(SEQ)[:, None]
    cols = jnp.arange(SEQ)[None, :]
    scores = jnp.where(cols <= rows, scores, -jnp.inf)
    top = lax.optimization_barrier(jnp.max(scores, axis=1, keepdims=True))
    lse = top[:, 0] + jnp.log(lax.optimization_barrier(jnp.sum(jnp.exp(scores - top), axis=1)))
    prob = jnp.exp(scores - lse[:, None])
    prob_b = prob.astype(jnp.bfloat16)
    out_b = jnp.dot(prob_b, values, preferred_element_type=jnp.float32).astype(jnp.bfloat16)
    return (out_b, prob, prob_b)

def forward_head(query, keys, values):
    return attend(query, keys, values)[0]

def backward_head(query, keys, values, grad, held, flag):
    scale = 1.0 / math.sqrt(HD)
    out_b, prob, prob_b = attend(query, keys, values)
    used = lax.optimization_barrier(jnp.where(flag, held, out_b))
    dprob = jnp.dot(grad, values.T, preferred_element_type=jnp.float32)
    delta = lax.optimization_barrier(jnp.sum(grad.astype(jnp.float32) * used.astype(jnp.float32), axis=1))
    dscore = (prob * (dprob - delta[:, None])).astype(jnp.bfloat16)
    dquery = (jnp.dot(dscore, keys, preferred_element_type=jnp.float32) * scale).astype(jnp.bfloat16)
    dkeys = jnp.dot(dscore.T, query, preferred_element_type=jnp.float32) * scale
    dvalues = jnp.dot(prob_b.T, grad, preferred_element_type=jnp.float32)
    return (dquery, dkeys, dvalues)

def forward_group(item):
    queries, keys, values = item
    return jax.vmap(forward_head, in_axes=(0, None, None))(queries, keys, values)

def backward_group(item):
    queries, keys, values, grads, helds, flag = item
    dquery, dkeys, dvalues = jax.vmap(backward_head, in_axes=(0, None, None, 0, 0, None))(queries, keys, values, grads, helds, flag)
    return (dquery, lax.optimization_barrier(jnp.sum(dkeys, axis=0)), lax.optimization_barrier(jnp.sum(dvalues, axis=0)))

def head_items(array):
    group = HEADS // KV_HEADS
    count = N_SECTION * MB * KV_HEADS
    return array.reshape(N_SECTION, MB, SEQ, KV_HEADS, group, HD).transpose(0, 1, 3, 4, 2, 5).reshape(count, group, SEQ, HD)

def head_full(items):
    group = HEADS // KV_HEADS
    return items.reshape(N_SECTION, MB, KV_HEADS, group, SEQ, HD).transpose(0, 1, 4, 2, 3, 5).reshape(N_SECTION, MB, SEQ, HEADS * HD)

def kv_items(array):
    count = N_SECTION * MB * KV_HEADS
    return array.reshape(N_SECTION, MB, SEQ, KV_HEADS, HD).transpose(0, 1, 3, 2, 4).reshape(count, SEQ, HD)

def kv_full(items):
    return items.reshape(N_SECTION, MB, KV_HEADS, SEQ, HD).transpose(0, 1, 3, 2, 4).reshape(N_SECTION, MB, SEQ, KV_HEADS * HD)

def reference(query, keys_values, grad_out, fwd_query, fwd_keys_values, held_out, evict):
    count = N_SECTION * MB * KV_HEADS
    half = N_SECTION // 2
    fwd_items = lax.map(forward_group, (head_items(fwd_query), kv_items(fwd_keys_values[:, :, 0]), kv_items(fwd_keys_values[:, :, 1])))
    fwd_out = head_full(fwd_items)
    bwd_flags = jnp.concatenate([evict[:, 1], jnp.zeros_like(evict[:, 1])], axis=0) == 1
    flag_items = jnp.broadcast_to(bwd_flags[:, :, None], (N_SECTION, MB, KV_HEADS)).reshape(count)
    held_src = held_out[::-1]
    dquery, dkeys, dvalues = lax.map(backward_group, (head_items(query), kv_items(keys_values[:, :, 0]), kv_items(keys_values[:, :, 1]), head_items(grad_out), head_items(held_src), flag_items))
    dq_full = head_full(dquery)
    grad_kv = jnp.stack([kv_full(dkeys), kv_full(dvalues)], axis=2).astype(jnp.bfloat16)
    passed_on = jnp.concatenate([jnp.zeros_like(fwd_out[:1]), fwd_out[:-1]], axis=0)
    fwd_flags = jnp.concatenate([evict[:, 0], jnp.zeros_like(evict[:, 0])], axis=0) == 1
    marked_out = jnp.where(fwd_flags[:, :, None, None], fwd_out, jnp.zeros_like(fwd_out))
    mirror_out = jnp.concatenate([jnp.zeros_like(marked_out[:half]), marked_out[:half][::-1]], axis=0)
    return (passed_on, dq_full, grad_kv, mirror_out)
```

```python
import math

import jax
import jax.numpy as jnp
from jax import lax
from jax.experimental import pallas as pl
from jax.experimental.pallas import tpu as pltpu
from jax.sharding import PartitionSpec as P

HD = 128
MASKED = -1e30


def dot_nt(a, b):
    return lax.dot_general(a, b, (((1,), (1,)), ((), ())), preferred_element_type=jnp.float32)


def dot_nn(a, b):
    return lax.dot_general(a, b, (((1,), (0,)), ((), ())), preferred_element_type=jnp.float32)


def head_pair(ref, pair):
    first = ref[0, :, 2 * pair * HD : (2 * pair + 1) * HD]
    second = ref[0, :, (2 * pair + 1) * HD : (2 * pair + 2) * HD]
    return jnp.concatenate([first, second], axis=0)


def forward_kernel(pos_ref, q_ref, k_ref, v_ref, out_ref):
    rows = q_ref.shape[1]
    keys = k_ref[...].reshape(-1, HD)
    values = v_ref[...].reshape(-1, HD)
    seq = keys.shape[0]
    wide = jnp.concatenate([values, jnp.ones_like(values)], axis=1)
    row = lax.broadcasted_iota(jnp.int32, (2 * rows, seq), 0) % rows + pos_ref[0] * rows
    col = lax.broadcasted_iota(jnp.int32, (2 * rows, seq), 1)
    bias = jnp.where(col <= row, 0.0, MASKED)
    factor = math.log2(math.e) / math.sqrt(HD)
    for pair in range(q_ref.shape[2] // (2 * HD)):
        scores = dot_nt(head_pair(q_ref, pair), keys) * factor + bias
        top = jnp.max(scores, axis=1, keepdims=True)
        weights = jnp.exp2(scores - top).astype(jnp.bfloat16)
        total = dot_nn(weights, wide)
        out = (total[:, :HD] / total[:, HD:]).astype(out_ref.dtype)
        out_ref[0, :, 2 * pair * HD : (2 * pair + 1) * HD] = out[:rows]
        out_ref[0, :, (2 * pair + 1) * HD : (2 * pair + 2) * HD] = out[rows:]


def backward_kernel(
    pos_ref, flag_ref, q_ref, k_ref, v_ref, g_ref, *others
):
    *held_refs, dq_ref, dkv_ref = others
    rows = q_ref.shape[1]
    keys = k_ref[...].reshape(-1, HD)
    values = v_ref[...].reshape(-1, HD)
    seq = keys.shape[0]
    keys_t = keys.T
    row = lax.broadcasted_iota(jnp.int32, (seq, 2 * rows), 1) % rows + pos_ref[0] * rows
    col = lax.broadcasted_iota(jnp.int32, (seq, 2 * rows), 0)
    bias = jnp.where(col <= row, 0.0, MASKED)
    scale = 1.0 / math.sqrt(HD)
    factor = math.log2(math.e) * scale
    use_held = flag_ref[0] == 1
    dkeys = jnp.zeros((seq, HD), jnp.float32)
    dvalues = jnp.zeros((seq, HD), jnp.float32)
    pairs = q_ref.shape[2] // (2 * HD)
    for pair in range(pairs):
        queries = head_pair(q_ref, pair)
        grads = head_pair(g_ref, pair)
        each = pairs // len(held_refs)
        held = head_pair(held_refs[pair // each].at[0], pair % each)
        product = grads.astype(jnp.float32) * held.astype(jnp.float32)
        delta_held = jnp.sum(product.T, axis=0, keepdims=True)
        scores = dot_nt(keys, queries) * factor + bias
        top = jnp.max(scores, axis=0, keepdims=True)
        weights = jnp.exp2(scores - top)
        prob = weights * (1.0 / jnp.sum(weights, axis=0, keepdims=True))
        dprob = dot_nt(values, grads)
        delta_own = jnp.sum(prob * dprob, axis=0, keepdims=True)
        delta = jnp.where(use_held, delta_held, delta_own)
        dscore = (prob * (dprob - delta)).astype(jnp.bfloat16)
        dvalues = dvalues + dot_nn(prob.astype(jnp.bfloat16), grads)
        dkeys = dkeys + dot_nn(dscore, queries)
        dquery = (dot_nn(keys_t, dscore) * scale).T.astype(dq_ref.dtype)
        dq_ref[0, :, 2 * pair * HD : (2 * pair + 1) * HD] = dquery[:rows]
        dq_ref[0, :, (2 * pair + 1) * HD : (2 * pair + 2) * HD] = dquery[rows:]
    blocks = dkv_ref.shape[0]
    dkv_ref[:, 0] = (dkeys * scale).reshape(blocks, rows, HD).astype(dkv_ref.dtype)
    dkv_ref[:, 1] = dvalues.reshape(blocks, rows, HD).astype(dkv_ref.dtype)


PARAMS = pltpu.CompilerParams(vmem_limit_bytes=48 * 2**20)


def forward_all(position, query, gathered):
    micro, rows, width = query.shape
    blocks = gathered.shape[0]
    kv_count = gathered.shape[4] // HD
    group = width // kv_count
    kv_block = (blocks, 1, 1, rows, HD)
    work = micro * rows * width * blocks * rows
    return pl.pallas_call(
        forward_kernel,
        grid_spec=pltpu.PrefetchScalarGridSpec(
            num_scalar_prefetch=1,
            grid=(micro, kv_count),
            in_specs=[
                pl.BlockSpec((1, rows, group), lambda m, g, pos: (m, 0, g)),
                pl.BlockSpec(kv_block, lambda m, g, pos: (0, m, 0, 0, g)),
                pl.BlockSpec(kv_block, lambda m, g, pos: (0, m, 1, 0, g)),
            ],
            out_specs=pl.BlockSpec((1, rows, group), lambda m, g, pos: (m, 0, g)),
        ),
        out_shape=jax.ShapeDtypeStruct(query.shape, query.dtype),
        compiler_params=PARAMS,
        cost_estimate=pl.CostEstimate(
            flops=8 * work, bytes_accessed=12 * 2**20, transcendentals=work // HD
        ),
        name="attention_forward",
    )(position, query, gathered, gathered)


def backward_one(index, position, flag, query, gathered, grad, held):
    _, rows, width = query.shape
    blocks = gathered.shape[0]
    kv_count = gathered.shape[4] // HD
    group = width // kv_count
    kv_block = (blocks, 1, 1, rows, HD)
    token_block = pl.BlockSpec((1, rows, group), lambda g, pos, flag: (index, 0, g))
    held_block = (1, 1, rows, held.shape[3])
    parts = group // held.shape[3]

    def held_map(part):
        return lambda g, pos, flag: (lax.rem(pos[0] - parts * g - part + blocks, blocks), index, 0, 0)

    work = rows * width * blocks * rows
    return pl.pallas_call(
        backward_kernel,
        grid_spec=pltpu.PrefetchScalarGridSpec(
            num_scalar_prefetch=2,
            grid=(kv_count,),
            in_specs=[
                token_block,
                pl.BlockSpec(kv_block, lambda g, pos, flag: (0, index, 0, 0, g)),
                pl.BlockSpec(kv_block, lambda g, pos, flag: (0, index, 1, 0, g)),
                token_block,
            ]
            + [pl.BlockSpec(held_block, held_map(part)) for part in range(parts)],
            out_specs=[
                pl.BlockSpec((1, rows, group), lambda g, pos, flag: (0, 0, g)),
                pl.BlockSpec((blocks, 2, rows, HD), lambda g, pos, flag: (0, 0, 0, g)),
            ],
        ),
        out_shape=[
            jax.ShapeDtypeStruct((1, rows, width), query.dtype),
            jax.ShapeDtypeStruct((blocks, 2, rows, kv_count * HD), jnp.bfloat16),
        ],
        compiler_params=PARAMS,
        cost_estimate=pl.CostEstimate(
            flops=20 * work, bytes_accessed=12 * 2**20, transcendentals=work // HD
        ),
        name="attention_backward",
    )(position, flag, query, gathered, gathered, grad, *[held] * parts)


def per_device(query, keys_values, grad_out, fwd_query, fwd_keys_values, held_out, evict):
    query = query[0]
    keys_values = keys_values[0]
    grad_out = grad_out[0]
    fwd_query = fwd_query[0]
    fwd_keys_values = fwd_keys_values[0]
    held_local = held_out[0]
    sections = lax.axis_size("section")
    width = lax.axis_size("tp")
    half = sections // 2
    section_pos = lax.axis_index("section")
    tp_pos = lax.axis_index("tp")
    micro, rows = query.shape[:2]
    columns = held_local.shape[2]
    position = tp_pos.astype(jnp.int32).reshape(1)

    fwd_all = lax.all_gather(fwd_keys_values, "tp")
    bwd_all = lax.all_gather(keys_values, "tp")

    def to_mirror(chunk, turn, senders):
        route = [
            (s * width + t, (sections - 1 - s) * width + (t + turn) % width)
            for s in senders
            for t in range(width)
        ]
        return lax.ppermute(chunk, ("section", "tp"), route)

    held_parts = []
    for turn in range(width):
        start = (tp_pos + turn) % width * rows
        chunk = lax.dynamic_slice_in_dim(held_local, start, rows, 1)
        held_parts.append(to_mirror(chunk, turn, range(half, sections)))
    held = jnp.stack(held_parts)

    early = section_pos < half
    flag_pair = lax.dynamic_index_in_dim(
        evict, jnp.minimum(section_pos, half - 1), 0, keepdims=False
    )
    fwd_marked = jnp.logical_and(early, flag_pair[0] == 1)
    bwd_marked = jnp.logical_and(early, flag_pair[1] == 1).astype(jnp.int32)

    out = forward_all(position, fwd_query, fwd_all)
    passed = lax.ppermute(out, "section", [(s, s + 1) for s in range(sections - 1)])
    mirror = jnp.zeros((micro, width * rows, columns), out.dtype)
    for turn in range(width):
        start = (tp_pos + turn) % width * columns
        chunk = lax.dynamic_slice_in_dim(out, start, columns, 2)
        chunk = jnp.where(fwd_marked[:, None, None], chunk, jnp.zeros_like(chunk))
        arrived = to_mirror(chunk, turn, range(half))
        place = (tp_pos - turn + width) % width * rows
        mirror = lax.dynamic_update_slice_in_dim(mirror, arrived, place, 1)

    dqs = []
    grads = []
    for index in range(micro):
        dquery, partial = backward_one(
            index, position, bwd_marked[index : index + 1], query, bwd_all, grad_out, held
        )
        dqs.append(dquery)
        grads.append(lax.psum_scatter(partial, "tp", scatter_dimension=0))
    return (passed[None], jnp.concatenate(dqs)[None], jnp.stack(grads)[None], mirror[None])


def solution(mesh):
    return jax.shard_map(
        per_device,
        mesh=mesh,
        in_specs=(
            P("section", None, "tp", None),
            P("section", None, None, "tp", None),
            P("section", None, "tp", None),
            P("section", None, "tp", None),
            P("section", None, None, "tp", None),
            P("section", None, None, "tp"),
            P(),
        ),
        out_specs=(
            P("section", None, "tp", None),
            P("section", None, "tp", None),
            P("section", None, None, "tp", None),
            P("section", None, None, "tp"),
        ),
        check_vma=False,
    )
```

```python
import math

import jax
import jax.numpy as jnp
from jax import lax
from jax.experimental import pallas as pl
from jax.experimental.pallas import tpu as pltpu
from jax.sharding import PartitionSpec as P

HD = 128
MASKED = -1e30


def dot_nt(a, b):
    return lax.dot_general(a, b, (((1,), (1,)), ((), ())), preferred_element_type=jnp.float32)


def dot_nn(a, b):
    return lax.dot_general(a, b, (((1,), (0,)), ((), ())), preferred_element_type=jnp.float32)


def head_pair(ref, pair):
    first = ref[0, :, 2 * pair * HD : (2 * pair + 1) * HD]
    second = ref[0, :, (2 * pair + 1) * HD : (2 * pair + 2) * HD]
    return jnp.concatenate([first, second], axis=0)


def attend_block(position, q_ref, k_ref, v_ref, out_ref):
    rows = q_ref.shape[1]
    keys = k_ref[...].reshape(-1, HD)
    values = v_ref[...].reshape(-1, HD)
    seq = keys.shape[0]
    wide = jnp.concatenate([values, jnp.ones_like(values)], axis=1)
    row = lax.broadcasted_iota(jnp.int32, (2 * rows, seq), 0) % rows + position * rows
    col = lax.broadcasted_iota(jnp.int32, (2 * rows, seq), 1)
    bias = jnp.where(col <= row, 0.0, MASKED)
    factor = math.log2(math.e) / math.sqrt(HD)
    for pair in range(q_ref.shape[2] // (2 * HD)):
        scores = dot_nt(head_pair(q_ref, pair), keys) * factor + bias
        top = jnp.max(scores, axis=1, keepdims=True)
        weights = jnp.exp2(scores - top).astype(jnp.bfloat16)
        total = dot_nn(weights, wide)
        out = (total[:, :HD] / total[:, HD:]).astype(out_ref.dtype)
        out_ref[0, :, 2 * pair * HD : (2 * pair + 1) * HD] = out[:rows]
        out_ref[0, :, (2 * pair + 1) * HD : (2 * pair + 2) * HD] = out[rows:]


def neighbours():
    me = lax.axis_index("tp")
    width = lax.axis_size("tp")
    level = me // 2
    pair = me + 1 - 2 * (me % 2)
    return me, level, width // 2, pair, (me + 2) % width, (me + width - 2) % width


def greet():
    _, level, levels, pair, up, down = neighbours()
    barrier = pltpu.get_barrier_semaphore()
    pl.semaphore_signal(barrier, inc=1, device_id={"tp": pair})

    @pl.when(level < levels - 1)
    def _():
        pl.semaphore_signal(barrier, inc=1, device_id={"tp": up})

    @pl.when(level > 0)
    def _():
        pl.semaphore_signal(barrier, inc=1, device_id={"tp": down})

    peers = 1 + jnp.minimum(level, 1) + jnp.minimum(levels - 1 - level, 1)
    pl.semaphore_wait(barrier, peers)


class Gather:
    def __init__(self, shard, full, sems):
        self.shard, self.full = shard, full
        self.local, self.up_send, self.up_recv, self.pair_send, self.pair_recv = sems
        self.me, self.level, self.levels, self.pair, self.up, _ = neighbours()
        self.micro = shard.shape[0]

    def copy(self, step, m, source, sends, recvs, target):
        first = self.me if source is None else source
        src = self.shard.at[m] if step == 0 and source is None else self.full.at[first - 2 * step, m]
        return pltpu.make_async_remote_copy(
            src_ref=src,
            dst_ref=self.full.at[first - 2 * step, m],
            send_sem=sends.at[step, m],
            recv_sem=recvs.at[step, m],
            device_id={"tp": target},
        )

    def to_up(self, step, m):
        return self.copy(step, m, None, self.up_send, self.up_recv, self.up)

    def from_down(self, step, m):
        return self.copy(step, m, self.me - 2, self.up_send, self.up_recv, self.up)

    def to_pair(self, step, m):
        return self.copy(step, m, None, self.pair_send, self.pair_recv, self.pair)

    def from_pair(self, step, m):
        return self.copy(step, m, self.pair, self.pair_send, self.pair_recv, self.pair)

    def fill(self, action):
        for place in range(2 * self.levels):

            @pl.when(jnp.logical_or(place == self.me, place // 2 > self.level))
            def _():
                copy = pltpu.make_async_copy(self.shard, self.full.at[place], self.local.at[place])
                copy.start() if action == "start" else copy.wait()

    def step(self, step):
        for m in range(self.micro):

            @pl.when(self.level >= step)
            def _():
                if step > 0:
                    self.from_down(step - 1, m).wait_recv()

                @pl.when(self.level < self.levels - 1)
                def _():
                    self.to_up(step, m).start()

                self.to_pair(step, m).start()

        if step == 0:
            self.fill("start")

    def finish(self):
        for step in range(self.levels):
            for m in range(self.micro):

                @pl.when(self.level >= step)
                def _():
                    self.from_pair(step, m).wait_recv()
                    self.to_pair(step, m).wait_send()

                    @pl.when(self.level < self.levels - 1)
                    def _():
                        self.to_up(step, m).wait_send()

        self.fill("wait")


def gather_scratch(micro):
    width = lax.axis_size("tp")
    steps = pltpu.SemaphoreType.DMA((width // 2, micro))
    return [pltpu.SemaphoreType.DMA((width,)), steps, steps, steps, steps]


def gather_kernel(shard_ref, full_ref, *sems):
    greet()
    gather = Gather(shard_ref, full_ref, sems)
    for step in range(gather.levels):
        gather.step(step)
    gather.finish()


def gather_all(shard):
    full = (lax.axis_size("tp"),) + shard.shape
    return pl.pallas_call(
        gather_kernel,
        in_specs=[pl.BlockSpec(memory_space=pl.ANY)],
        out_specs=pl.BlockSpec(memory_space=pl.ANY),
        out_shape=jax.ShapeDtypeStruct(full, shard.dtype),
        scratch_shapes=gather_scratch(shard.shape[0]),
        compiler_params=pltpu.CompilerParams(collective_id=0, has_side_effects=True),
        name="gather_keys_values",
    )(shard)


def forward_kernel(q_ref, k_ref, v_ref, shard_ref, out_ref, full_ref, *sems):
    now = pl.program_id(0) * pl.num_programs(1) + pl.program_id(1)
    micro = shard_ref.shape[0]
    total = micro * (shard_ref.shape[3] // HD)
    gather = Gather(shard_ref, full_ref, sems)

    @pl.when(now == 0)
    def _():
        greet()

    for step in range(gather.levels):

        @pl.when(now == step * total // gather.levels)
        def _():
            gather.step(step)

    attend_block(gather.me, q_ref, k_ref, v_ref, out_ref)

    @pl.when(now == total - 1)
    def _():
        gather.finish()


def scatter_kernel(*refs):
    (
        *parts, out_ref, pair_in, up_in, staged, total,
        pair_send, pair_recv, down_send, down_recv,
    ) = refs
    me, level, levels, pair, _, down = neighbours()
    side = me % 2
    micro = len(parts)
    greet()

    def to_pair(place, m):
        return pltpu.make_async_remote_copy(
            src_ref=parts[m].at[2 * place + 1 - side],
            dst_ref=pair_in.at[place, m],
            send_sem=pair_send.at[place, m],
            recv_sem=pair_recv.at[place, m],
            device_id={"tp": pair},
        )

    def to_down(place, m):
        return pltpu.make_async_remote_copy(
            src_ref=staged.at[place, m],
            dst_ref=up_in.at[place, m],
            send_sem=down_send.at[place, m],
            recv_sem=down_recv.at[place, m],
            device_id={"tp": down},
        )

    for place in range(levels):
        for m in range(micro):

            @pl.when(level >= place)
            def _():
                to_pair(place, m).start()

    for place in range(levels):
        for m in range(micro):

            @pl.when(level >= place)
            def _():
                to_pair(place, m).wait_recv()
                own = parts[m][2 * place + side].astype(jnp.float32)
                total[...] = own + pair_in[place, m].astype(jnp.float32)

                @pl.when(level < levels - 1)
                def _():
                    to_down(place, m).wait_recv()
                    total[...] += up_in[place, m].astype(jnp.float32)

                @pl.when(level > place)
                def _():
                    staged[place, m] = total[...].astype(staged.dtype)
                    to_down(place, m).start()

                @pl.when(level == place)
                def _():
                    out_ref[m] = total[...].astype(out_ref.dtype)

    for place in range(levels):
        for m in range(micro):

            @pl.when(level >= place)
            def _():
                to_pair(place, m).wait_send()

            @pl.when(level > place)
            def _():
                to_down(place, m).wait_send()


def scatter_sum(parts):
    micro = len(parts)
    levels = parts[0].shape[0] // 2
    block = parts[0].shape[1:]
    slots = pltpu.VMEM((levels, micro) + block, jnp.bfloat16)
    steps = pltpu.SemaphoreType.DMA((levels, micro))
    return pl.pallas_call(
        scatter_kernel,
        in_specs=[pl.BlockSpec(memory_space=pltpu.VMEM)] * micro,
        out_specs=pl.BlockSpec(memory_space=pltpu.VMEM),
        out_shape=jax.ShapeDtypeStruct((micro,) + block, jnp.bfloat16),
        scratch_shapes=[slots, slots, slots, pltpu.VMEM(block, jnp.float32)] + [steps] * 4,
        compiler_params=pltpu.CompilerParams(
            collective_id=2, has_side_effects=True, vmem_limit_bytes=32 * 2**20
        ),
        name="scatter_gradients",
    )(*parts)


def backward_kernel(
    pos_ref, flag_ref, q_ref, k_ref, v_ref, g_ref, *others
):
    *held_refs, dq_ref, dkv_ref = others
    rows = q_ref.shape[1]
    keys = k_ref[...].reshape(-1, HD)
    values = v_ref[...].reshape(-1, HD)
    seq = keys.shape[0]
    keys_t = keys.T
    row = lax.broadcasted_iota(jnp.int32, (seq, 2 * rows), 1) % rows + pos_ref[0] * rows
    col = lax.broadcasted_iota(jnp.int32, (seq, 2 * rows), 0)
    bias = jnp.where(col <= row, 0.0, MASKED)
    scale = 1.0 / math.sqrt(HD)
    factor = math.log2(math.e) * scale
    use_held = flag_ref[0] == 1
    dkeys = jnp.zeros((seq, HD), jnp.float32)
    dvalues = jnp.zeros((seq, HD), jnp.float32)
    pairs = q_ref.shape[2] // (2 * HD)
    for pair in range(pairs):
        queries = head_pair(q_ref, pair)
        grads = head_pair(g_ref, pair)
        each = pairs // len(held_refs)
        held = head_pair(held_refs[pair // each].at[0], pair % each)
        product = grads.astype(jnp.float32) * held.astype(jnp.float32)
        delta_held = jnp.sum(product.T, axis=0, keepdims=True)
        scores = dot_nt(keys, queries) * factor + bias
        top = jnp.max(scores, axis=0, keepdims=True)
        weights = jnp.exp2(scores - top)
        prob = weights * (1.0 / jnp.sum(weights, axis=0, keepdims=True))
        dprob = dot_nt(values, grads)
        delta_own = jnp.sum(prob * dprob, axis=0, keepdims=True)
        delta = jnp.where(use_held, delta_held, delta_own)
        dscore = (prob * (dprob - delta)).astype(jnp.bfloat16)
        dvalues = dvalues + dot_nn(prob.astype(jnp.bfloat16), grads)
        dkeys = dkeys + dot_nn(dscore, queries)
        dquery = (dot_nn(keys_t, dscore) * scale).T.astype(dq_ref.dtype)
        dq_ref[0, :, 2 * pair * HD : (2 * pair + 1) * HD] = dquery[:rows]
        dq_ref[0, :, (2 * pair + 1) * HD : (2 * pair + 2) * HD] = dquery[rows:]
    blocks = dkv_ref.shape[0]
    dkv_ref[:, 0] = (dkeys * scale).reshape(blocks, rows, HD).astype(dkv_ref.dtype)
    dkv_ref[:, 1] = dvalues.reshape(blocks, rows, HD).astype(dkv_ref.dtype)


PARAMS = pltpu.CompilerParams(vmem_limit_bytes=48 * 2**20)


def forward_all(query, gathered, shard):
    micro, rows, width = query.shape
    blocks = gathered.shape[0]
    kv_count = gathered.shape[4] // HD
    group = width // kv_count
    kv_block = (blocks, 1, 1, rows, HD)
    work = micro * rows * width * blocks * rows
    return pl.pallas_call(
        forward_kernel,
        grid=(micro, kv_count),
        in_specs=[
            pl.BlockSpec((1, rows, group), lambda m, g: (m, 0, g)),
            pl.BlockSpec(kv_block, lambda m, g: (0, m, 0, 0, g)),
            pl.BlockSpec(kv_block, lambda m, g: (0, m, 1, 0, g)),
            pl.BlockSpec(memory_space=pl.ANY),
        ],
        out_specs=[
            pl.BlockSpec((1, rows, group), lambda m, g: (m, 0, g)),
            pl.BlockSpec(memory_space=pl.ANY),
        ],
        out_shape=[
            jax.ShapeDtypeStruct(query.shape, query.dtype),
            jax.ShapeDtypeStruct((blocks,) + shard.shape, shard.dtype),
        ],
        scratch_shapes=gather_scratch(micro),
        compiler_params=pltpu.CompilerParams(
            collective_id=1, has_side_effects=True, vmem_limit_bytes=48 * 2**20
        ),
        cost_estimate=pl.CostEstimate(
            flops=8 * work, bytes_accessed=12 * 2**20, transcendentals=work // HD
        ),
        name="attention_forward",
    )(query, gathered, gathered, shard)


def backward_one(index, position, flag, query, gathered, grad, held):
    _, rows, width = query.shape
    blocks = gathered.shape[0]
    kv_count = gathered.shape[4] // HD
    group = width // kv_count
    kv_block = (blocks, 1, 1, rows, HD)
    token_block = pl.BlockSpec((1, rows, group), lambda g, pos, flag: (index, 0, g))
    held_block = (1, 1, rows, held.shape[3])
    parts = group // held.shape[3]

    def held_map(part):
        return lambda g, pos, flag: (lax.rem(pos[0] - parts * g - part + blocks, blocks), index, 0, 0)

    work = rows * width * blocks * rows
    return pl.pallas_call(
        backward_kernel,
        grid_spec=pltpu.PrefetchScalarGridSpec(
            num_scalar_prefetch=2,
            grid=(kv_count,),
            in_specs=[
                token_block,
                pl.BlockSpec(kv_block, lambda g, pos, flag: (0, index, 0, 0, g)),
                pl.BlockSpec(kv_block, lambda g, pos, flag: (0, index, 1, 0, g)),
                token_block,
            ]
            + [pl.BlockSpec(held_block, held_map(part)) for part in range(parts)],
            out_specs=[
                pl.BlockSpec((1, rows, group), lambda g, pos, flag: (0, 0, g)),
                pl.BlockSpec((blocks, 2, rows, HD), lambda g, pos, flag: (0, 0, 0, g)),
            ],
        ),
        out_shape=[
            jax.ShapeDtypeStruct((1, rows, width), query.dtype),
            jax.ShapeDtypeStruct((blocks, 2, rows, kv_count * HD), jnp.bfloat16),
        ],
        compiler_params=PARAMS,
        cost_estimate=pl.CostEstimate(
            flops=20 * work, bytes_accessed=12 * 2**20, transcendentals=work // HD
        ),
        name="attention_backward",
    )(position, flag, query, gathered, gathered, grad, *[held] * parts)


def per_device(query, keys_values, grad_out, fwd_query, fwd_keys_values, held_out, evict):
    query = query[0]
    keys_values = keys_values[0]
    grad_out = grad_out[0]
    fwd_query = fwd_query[0]
    fwd_keys_values = fwd_keys_values[0]
    held_local = held_out[0]
    sections = lax.axis_size("section")
    width = lax.axis_size("tp")
    half = sections // 2
    section_pos = lax.axis_index("section")
    tp_pos = lax.axis_index("tp")
    micro, rows = query.shape[:2]
    columns = held_local.shape[2]
    position = tp_pos.astype(jnp.int32).reshape(1)

    fwd_all = gather_all(fwd_keys_values)

    def to_mirror(chunk, turn, senders):
        route = [
            (s * width + t, (sections - 1 - s) * width + (t + turn) % width)
            for s in senders
            for t in range(width)
        ]
        return lax.ppermute(chunk, ("section", "tp"), route)

    held_parts = []
    for turn in range(width):
        start = (tp_pos + turn) % width * rows
        chunk = lax.dynamic_slice_in_dim(held_local, start, rows, 1)
        held_parts.append(to_mirror(chunk, turn, range(half, sections)))
    held = jnp.stack(held_parts)

    early = section_pos < half
    flag_pair = lax.dynamic_index_in_dim(
        evict, jnp.minimum(section_pos, half - 1), 0, keepdims=False
    )
    fwd_marked = jnp.logical_and(early, flag_pair[0] == 1)
    bwd_marked = jnp.logical_and(early, flag_pair[1] == 1).astype(jnp.int32)

    out, bwd_all = forward_all(fwd_query, fwd_all, keys_values)
    passed = lax.ppermute(out, "section", [(s, s + 1) for s in range(sections - 1)])
    mirror = jnp.zeros((micro, width * rows, columns), out.dtype)
    for turn in range(width):
        start = (tp_pos + turn) % width * columns
        chunk = lax.dynamic_slice_in_dim(out, start, columns, 2)
        chunk = jnp.where(fwd_marked[:, None, None], chunk, jnp.zeros_like(chunk))
        arrived = to_mirror(chunk, turn, range(half))
        place = (tp_pos - turn + width) % width * rows
        mirror = lax.dynamic_update_slice_in_dim(mirror, arrived, place, 1)

    dqs = []
    grads = []
    for index in range(micro):
        dquery, partial = backward_one(
            index, position, bwd_marked[index : index + 1], query, bwd_all, grad_out, held
        )
        dqs.append(dquery)
        grads.append(partial)
    return (passed[None], jnp.concatenate(dqs)[None], scatter_sum(grads)[None], mirror[None])


def solution(mesh):
    return jax.shard_map(
        per_device,
        mesh=mesh,
        in_specs=(
            P("section", None, "tp", None),
            P("section", None, None, "tp", None),
            P("section", None, "tp", None),
            P("section", None, "tp", None),
            P("section", None, None, "tp", None),
            P("section", None, None, "tp"),
            P(),
        ),
        out_specs=(
            P("section", None, "tp", None),
            P("section", None, "tp", None),
            P("section", None, None, "tp", None),
            P("section", None, None, "tp"),
        ),
        check_vma=False,
    )
```
